32 devices in a mesh: centre: 8 (over z, y), row: 4 (over x, core).
Axes of the slice: x: 2, y: 2, z: 4, core: 2. Of those that a mesh axis runs over, the one named last changes fastest.
Arguments:
- pool: bfloat16 [1024, 16384], P('centre', 'row')
- batch_index: int32 [1024], P('row'), may hold values from 0 to 16383, as said below
- targets: float32 [10, 1024], P(None, 'row'), may hold values from -6 to 6
- centres: bfloat16 [65536, 1024], P(('centre', 'row'))
- weights: float32 [10, 65536], P(None, ('centre', 'row')), may hold values from -0.0234375 to 0.0234375
- sample_index: int32 [512], P(('centre', 'row')), may hold values from 0 to 65535, as said below
- factor: float32 [512, 128], P(('centre', 'row')), may hold values from -0.5 to 0.5
Outputs:
- gradient: float32 [10, 1024], P(None, 'row')
- update: float32 [10, 512], P(None, ('centre', 'row'))
The draws below stay inside these ranges and needn't reach their ends.
Inputs may be any that keep to these rules, and one draw needn't show every extreme that they name: `batch_index`: the entries at positions r * 256 to (r + 1) * 256 - 1 lie in r * 4096 to (r + 1) * 4096 - 1; repeats may occur. `sample_index`: all entries differ; the entries at positions k * 16 to (k + 1) * 16 - 1 lie in k * 2048 to (k + 1) * 2048 - 1.
All inputs are finite; a program needn't handle non-finite values.
Results may differ from the reference program's by a relative error of at most 0.0003.
Values may be sent and summed in bfloat16 or wider, within the bound.
A program may use at most 128 MiB of HBM per device.

```python
import math
import jax
import jax.numpy as jnp
from jax import lax

D = 1024
L = 10
Q = 128
PROJ_STEPS = 2
B_DEV = 256
M_DEV = 2048
SAMP_DEV = 16
POOL_DEV = 4096
B = 1024
M = 65536
S = 512
POOL = 16384


def embed_rows(base, salt, count):
    directions = jax.random.normal(jax.random.fold_in(base, 101), (64, D), jnp.float32)
    key = jax.random.fold_in(base, salt)
    key_pick, key_strength, key_noise, key_scale = jax.random.split(key, 4)
    picks = jax.random.randint(key_pick, (count,), 0, 64)
    strength = jax.random.uniform(key_strength, (count, 1), jnp.float32, 0.0, 2.0)
    noise = jax.random.normal(key_noise, (count, D), jnp.float32)
    scale = jnp.exp(jax.random.uniform(key_scale, (count, 1), jnp.float32, -0.6931472, 0.6931472))
    return (noise + strength * directions[picks]) * scale


def draw_pool(key, part):
    return embed_rows(key, 1, POOL).T.astype(jnp.bfloat16)


def draw_centres(key, part):
    return embed_rows(key, 2, M).astype(jnp.bfloat16)


def draw_batch_index(key, part):
    groups = B // B_DEV
    local = jax.random.randint(key, (groups, B_DEV), 0, POOL_DEV).astype(jnp.int32)
    local = local.at[0, 0].set(0)
    local = local.at[groups - 1, B_DEV - 1].set(POOL_DEV - 1)
    offsets = jnp.arange(groups, dtype=jnp.int32)[:, None] * POOL_DEV
    return (local + offsets).reshape(B).astype(jnp.int32)


def draw_sample_index(key, part):
    blocks = S // SAMP_DEV
    keys = jax.random.split(key, blocks)
    perms = jax.vmap(lambda one: jax.random.permutation(one, M_DEV))(keys).astype(jnp.int32)
    block_ids = jnp.arange(blocks, dtype=jnp.int32)
    target = jnp.where(block_ids == 0, 0, jnp.where(block_ids == blocks - 1, M_DEV - 1, perms[:, 0]))
    shift = (target - perms[:, 0])[:, None]
    local = (perms[:, :SAMP_DEV] + shift + M_DEV) % M_DEV
    offsets = block_ids[:, None] * M_DEV
    return (local + offsets).reshape(S).astype(jnp.int32)


def steps_of(rng, extent, shards, smallest, top_value):
    loudness, own = 1.0, jax.random.fold_in(rng, 6)
    for axis_at, parts in shards:
        heights = jnp.exp(jax.random.uniform(jax.random.fold_in(own, axis_at), (parts,), jnp.float32, smallest / len(shards), top_value / len(shards)))
        loudness = loudness * jnp.repeat(heights, extent[axis_at] // parts).reshape([-1 if axis == axis_at else 1 for axis in range(len(extent))])
    return loudness


def centred(own_key, shape, deviation, bound, cuts=(), held_as=jnp.bfloat16):
    array = jax.random.normal(own_key, shape, jnp.float32) * deviation
    if len(cuts) > 0:
        array = steps_of(own_key, shape, cuts, -0.22, 0.18) * array
    return jnp.clip(array, min=-bound, max=bound).astype(held_as)


def setup_inputs(seed: int = 0) -> dict:
    key_of = jax.random.split(jax.random.key(seed), 8)
    pool = draw_pool(jax.random.fold_in(key_of[7], 71), 0)
    batch_index = draw_batch_index(jax.random.fold_in(key_of[7], 71), 0)
    targets = centred(key_of[2], (L, B), 1.0, 6.0, ((1, 4),), jnp.float32)
    centres = draw_centres(jax.random.fold_in(key_of[7], 71), 0)
    weights = centred(key_of[4], (L, M), M ** -0.5, 0.0234375, ((1, 32),), jnp.float32)
    sample_index = draw_sample_index(jax.random.fold_in(key_of[7], 71), 0)
    factor = centred(key_of[6], (S, Q), (S // 4) ** -0.5, 0.5, ((0, 32),), jnp.float32)
    return dict(pool=pool, batch_index=batch_index, targets=targets, centres=centres, weights=weights, sample_index=sample_index, factor=factor)


EPS = 1e-06
HIGH = lax.Precision.HIGHEST

def row_scale(rows, axis):
    values = rows.astype(jnp.float32)
    return jnp.sqrt(lax.optimization_barrier(jnp.mean(values * values, axis=axis)) + EPS)

def tangent_kernel(inner, left_scale, right_scale, width):
    product = left_scale[:, None] * right_scale[None, :]
    cosine = jnp.clip(inner / (width * product), -1.0, 1.0)
    angle = jnp.arccos(cosine)
    first = (math.pi - angle) / math.pi
    second = (cosine * (math.pi - angle) + jnp.sqrt(1.0 - cosine * cosine)) / math.pi
    return product * (second + cosine * first)

def reference(pool, batch_index, targets, centres, weights, sample_index, factor):
    width = float(D)
    batch = jnp.take(pool, batch_index, axis=1)
    batch_scale = row_scale(batch, 0)
    centre_scale = row_scale(centres, 1)
    blocks = M // M_DEV

    def add_block(total, index):
        start = index * M_DEV
        rows = lax.dynamic_slice_in_dim(centres, start, M_DEV, 0)
        scales = lax.dynamic_slice_in_dim(centre_scale, start, M_DEV, 0)
        coeffs = lax.dynamic_slice_in_dim(weights, start, M_DEV, 1)
        inner = jnp.dot(rows, batch, preferred_element_type=jnp.float32)
        kernel = tangent_kernel(inner, scales, batch_scale, width)
        return (total + jnp.dot(coeffs, kernel, precision=HIGH), None)
    predictions, _ = lax.scan(add_block, jnp.zeros((L, B), jnp.float32), jnp.arange(blocks, dtype=jnp.int32))
    gradient = predictions - targets
    sample = jnp.take(centres, sample_index, axis=0)
    sample_scale = jnp.take(centre_scale, sample_index)
    cross = tangent_kernel(jnp.dot(sample, batch, preferred_element_type=jnp.float32), sample_scale, batch_scale, width)
    push = lax.dot_general(gradient, cross, (((1,), (1,)), ((), ())), precision=HIGH) / B
    inner = lax.dot_general(sample, sample, (((1,), (1,)), ((), ())), preferred_element_type=jnp.float32)
    gram = tangent_kernel(inner, sample_scale, sample_scale, width)
    update = jnp.zeros((L, S), jnp.float32)
    for step in range(PROJ_STEPS):
        slope = jnp.dot(update, gram, precision=HIGH) / S + push
        coef = jnp.dot(slope, factor, precision=HIGH)
        update = update - (slope - jnp.dot(coef, factor.T, precision=HIGH))
    return (gradient, update)
```

```python
import functools
import math

import jax
import jax.numpy as jnp
from jax import lax
from jax.experimental import pallas as pl
from jax.experimental.pallas import tpu as pltpu
from jax.sharding import PartitionSpec as P

PROJ_STEPS = 2
EPS = 1e-06
HIGH = lax.Precision.HIGHEST
MESH = pl.DeviceIdType.MESH
CONTRACT = (((1,), (1,)), ((), ()))
VMEM = pl.BlockSpec(memory_space=pltpu.VMEM)
POLY = (0.3183098802, -0.8408441305, 0.09680761083, -0.03656900053,
        0.01880055716, -0.00968401399, 0.003746990699, -0.0007261497719)


def row_scale(rows, axis):
    values = rows.astype(jnp.float32)
    return jnp.sqrt(jnp.mean(values * values, axis=axis) + EPS)


def arc(cosine):
    size = jnp.minimum(jnp.abs(cosine), 1.0)
    rest = 1.0 - size
    root = rest * lax.rsqrt(jnp.maximum(rest, 1e-30))
    value = jnp.full_like(size, POLY[-1])
    for factor in POLY[-2::-1]:
        value = value * size + factor
    linear = jnp.minimum(jnp.maximum(cosine, 0.0), 1.0)
    return root * value + (linear + linear)


def pick_kernel(pool_ref, index_ref, out_ref):
    count = index_ref.shape[1]
    depth = pool_ref.shape[1]
    tile = 512
    total = jnp.zeros(out_ref.shape, jnp.float32)
    for start in range(0, depth, tile):
        size = min(tile, depth - start)
        wanted = index_ref[...] - start
        hot = lax.broadcasted_iota(jnp.int32, (size, count), 0) == wanted
        total += jnp.dot(pool_ref[:, start:start + size], hot.astype(jnp.bfloat16),
                         preferred_element_type=jnp.float32)
    out_ref[...] = total.astype(out_ref.dtype)


def gather_kernel(groups, rows, count, *refs):
    ins, outs = refs[:count], refs[count:2 * count]
    (own, send1, recv1, send2, recv2, send3, recv3) = refs[2 * count:]
    pairs = rows // 2
    c = lax.axis_index("centre")
    r = lax.axis_index("row")
    x, core = r // 2, r % 2
    other = r + 1 - 2 * core

    barrier = pltpu.get_barrier_semaphore()
    for d in range(1, groups):
        pl.semaphore_signal(barrier, inc=1, device_id=((c + d) % groups, r), device_id_type=MESH)
    for d in range(1, pairs):
        pl.semaphore_signal(barrier, inc=1, device_id=(c, ((x + d) % pairs) * 2 + core), device_id_type=MESH)
    pl.semaphore_signal(barrier, inc=1, device_id=(c, other), device_id_type=MESH)
    pl.semaphore_wait(barrier, groups - 1 + pairs - 1 + 1)

    def slot(a, row, centre):
        size = ins[a].shape[0]
        return outs[a].at[row, pl.ds(pl.multiple_of(centre * size, size), size), :]

    sent = []
    for a in range(count):
        for d in range(1, groups):
            to = (c + d) % groups
            copy = pltpu.make_async_remote_copy(
                ins[a], slot(a, r, c), send1.at[a, d], recv1.at[a, d],
                device_id=(to, r), device_id_type=MESH)
            copy.start()
            sent.append(copy)
    keep = []
    for a in range(count):
        copy = pltpu.make_async_copy(ins[a], slot(a, r, c), own.at[a])
        copy.start()
        keep.append(copy)
    for copy in keep:
        copy.wait()

    def forward(a, row, d, x_step):
        place = slot(a, row, (c + groups - d) % groups)
        copy = pltpu.make_async_remote_copy(
            place, place, send3.at[a, x_step, d], recv3.at[a, x_step, d],
            device_id=(c, other), device_id_type=MESH)
        copy.start()
        sent.append(copy)

    for a in range(count):
        for d in range(groups):
            place = slot(a, r, (c + groups - d) % groups)
            if d:
                pltpu.make_async_remote_copy(
                    ins[a], place, send1.at[a, d], recv1.at[a, d],
                    device_id=(c, r), device_id_type=MESH).wait_recv()
            for e in range(1, pairs):
                copy = pltpu.make_async_remote_copy(
                    place, place, send2.at[a, e, d], recv2.at[a, e, d],
                    device_id=(c, ((x + e) % pairs) * 2 + core), device_id_type=MESH)
                copy.start()
                sent.append(copy)
            forward(a, r, d, 0)
    for a in range(count):
        for d in range(groups):
            for e in range(1, pairs):
                row = ((x + pairs - e) % pairs) * 2 + core
                place = slot(a, row, (c + groups - d) % groups)
                pltpu.make_async_remote_copy(
                    place, place, send2.at[a, e, d], recv2.at[a, e, d],
                    device_id=(c, r), device_id_type=MESH).wait_recv()
                forward(a, row, d, e)
    for a in range(count):
        for d in range(groups):
            for e in range(pairs):
                row = ((x + pairs - e) % pairs) * 2 + (1 - core)
                place = slot(a, row, (c + groups - d) % groups)
                pltpu.make_async_remote_copy(
                    place, place, send3.at[a, e, d], recv3.at[a, e, d],
                    device_id=(c, r), device_id_type=MESH).wait_recv()
    for copy in sent:
        copy.wait_send()


def gather_all(groups, rows, arrays):
    count = len(arrays)
    pairs = rows // 2
    dma = pltpu.SemaphoreType.DMA
    return pl.pallas_call(
        functools.partial(gather_kernel, groups, rows, count),
        out_shape=[jax.ShapeDtypeStruct((rows, groups * a.shape[0], a.shape[1]), a.dtype) for a in arrays],
        in_specs=[VMEM] * count,
        out_specs=[VMEM] * count,
        scratch_shapes=[
            dma((count,)),
            dma((count, groups)), dma((count, groups)),
            dma((count, pairs, groups)), dma((count, pairs, groups)),
            dma((count, pairs, groups)), dma((count, pairs, groups)),
        ],
        compiler_params=pltpu.CompilerParams(
            collective_id=0, has_side_effects=True, vmem_limit_bytes=48 << 20),
    )(*arrays)


def main_kernel(tile, cent_ref, inv_ref, weight_ref, batch_ref, bscale_ref, samp_ref, sinv_ref, sscale_ref,
                part_ref, cross_ref):
    bscale = bscale_ref[0]
    binv = 1.0 / bscale
    batch = batch_ref[0]
    half = weight_ref.shape[0]
    first = jnp.zeros((2 * half, batch.shape[1]), jnp.float32)
    second = jnp.zeros((half, batch.shape[1]), jnp.float32)
    for start in range(0, cent_ref.shape[0], tile):
        inner = jnp.dot(cent_ref[start:start + tile, :], batch, preferred_element_type=jnp.float32)
        value = arc(inner * inv_ref[start:start + tile, :] * binv)
        high = value.astype(jnp.bfloat16)
        low = (value - high.astype(jnp.float32)).astype(jnp.bfloat16)
        exact = weight_ref[:, start:start + tile]
        upper = exact.astype(jnp.bfloat16)
        lower = (exact - upper.astype(jnp.float32)).astype(jnp.bfloat16)
        coeffs = jnp.concatenate([upper, lower], axis=0)
        first += jnp.dot(coeffs, high, preferred_element_type=jnp.float32)
        second += jnp.dot(upper, low, preferred_element_type=jnp.float32)
    part_ref[0] = (first[:half] + (first[half:] + second)) * bscale
    count = samp_ref.shape[0]
    step = min(tile, count)
    for start in range(0, count, step):
        inner = jnp.dot(samp_ref[start:start + step, :], batch, preferred_element_type=jnp.float32)
        value = arc(inner * sinv_ref[start:start + step, :] * binv)
        cross_ref[0, start:start + step, :] = value * (sscale_ref[start:start + step, :] * bscale)


def gram_kernel(left_ref, linv_ref, lscale_ref, right_ref, rscale_ref, out_ref):
    inner = lax.dot_general(left_ref[...], right_ref[...], CONTRACT, preferred_element_type=jnp.float32)
    rscale = rscale_ref[...]
    value = arc(inner * linv_ref[...] * (1.0 / rscale))
    out_ref[...] = value * (lscale_ref[...] * rscale)


def sum_kernel(groups, rows, part_ref, target_ref, grad_ref, all_ref, buf1, buf2, mine,
               send1, recv1, send2, recv2, send3, recv3):
    c = lax.axis_index("centre")
    r = lax.axis_index("row")
    barrier = pltpu.get_barrier_semaphore()
    for d in range(1, rows):
        pl.semaphore_signal(barrier, inc=1, device_id=(c, (r + d) % rows), device_id_type=MESH)
    for d in range(1, groups):
        pl.semaphore_signal(barrier, inc=1, device_id=((c + d) % groups, r), device_id_type=MESH)
    pl.semaphore_wait(barrier, rows - 1 + groups - 1)
    sent = []

    def move(src, dst, send, recv, to):
        copy = pltpu.make_async_remote_copy(src, dst, send, recv, device_id=to, device_id_type=MESH)
        copy.start()
        sent.append(copy)

    def landed(dst, send, recv):
        pltpu.make_async_remote_copy(dst, dst, send, recv, device_id=(c, r), device_id_type=MESH).wait_recv()

    for d in range(1, rows):
        to = (r + d) % rows
        move(part_ref.at[to], buf1.at[d], send1.at[d], recv1.at[d], (c, to))
    total = part_ref[r]
    for d in range(1, rows):
        landed(buf1.at[d], send1.at[d], recv1.at[d])
        total += buf1[d]
    mine[...] = total
    for d in range(1, groups):
        move(mine, buf2.at[c], send2.at[d], recv2.at[d], ((c + d) % groups, r))
    for d in range(1, groups):
        place = buf2.at[(c + groups - d) % groups]
        landed(place, send2.at[d], recv2.at[d])
    buf2[c] = total
    total = buf2[0]
    for d in range(1, groups):
        total += buf2[d]
    grad = total - target_ref[...]
    grad_ref[...] = grad
    all_ref[r] = grad
    for d in range(1, rows):
        move(grad_ref, all_ref.at[r], send3.at[d], recv3.at[d], (c, (r + d) % rows))
    for d in range(1, rows):
        landed(all_ref.at[(r + rows - d) % rows], send3.at[d], recv3.at[d])
    for copy in sent:
        copy.wait_send()


def on_device(pool, batch_index, targets, centres, weights, sample_index, factor):
    width = float(centres.shape[1])
    labels = weights.shape[0]
    rows_dev = batch_index.shape[0]
    pool_dev = pool.shape[1]
    cent_dev = centres.shape[0]
    samp_dev = sample_index.shape[0]
    rows = lax.axis_size("row")
    groups = lax.axis_size("centre")
    total_rows = rows_dev * rows
    total_samp = samp_dev * rows * groups
    whole = total_samp <= 1024
    half = -(-labels // 16) * 16
    params = pltpu.CompilerParams(vmem_limit_bytes=48 << 20)

    local_batch = batch_index - lax.axis_index("row") * pool_dev
    picked = pl.pallas_call(
        pick_kernel,
        out_shape=jax.ShapeDtypeStruct((pool.shape[0], rows_dev), pool.dtype),
        compiler_params=params,
    )(pool, local_batch[None, :])
    local_sample = sample_index - lax.axis_index(("centre", "row")) * cent_dev
    sample_rows = jnp.take(centres, local_sample, axis=0)
    arrays = [picked, sample_rows] + ([factor] if whole else [])
    gathered = gather_all(groups, rows, arrays)
    batch = gathered[0]
    samples = gathered[1].reshape(total_samp, -1)

    centre_scale = row_scale(centres, 1)
    scaled = jnp.pad(weights * centre_scale[None, :], ((0, half - labels), (0, 0)))
    inv = (1.0 / (width * centre_scale))[:, None]
    bscale = row_scale(batch, 1)[:, None, :]
    sscale = row_scale(samples, 1)
    left = samples if whole else sample_rows
    lscale = (sscale if whole else row_scale(sample_rows, 1))[:, None]
    linv = 1.0 / (width * lscale)
    extra = left.shape[0]
    fixed = lambda shape: pl.BlockSpec(shape, lambda i: (0, 0))
    moving = lambda a, b: pl.BlockSpec((1, a, b), lambda i: (i, 0, 0))
    partial, cross = pl.pallas_call(
        functools.partial(main_kernel, 256),
        grid=(rows,),
        out_shape=[jax.ShapeDtypeStruct((rows, half, rows_dev), jnp.float32),
                   jax.ShapeDtypeStruct((rows, extra, rows_dev), jnp.float32)],
        in_specs=[fixed(centres.shape), fixed(inv.shape), fixed(scaled.shape),
                  moving(batch.shape[1], rows_dev), moving(1, rows_dev),
                  fixed(left.shape), fixed(linv.shape), fixed(lscale.shape)],
        out_specs=[moving(half, rows_dev), moving(extra, rows_dev)],
        compiler_params=params,
    )(centres, inv, scaled, batch, bscale, left, linv, lscale)
    tile = min(512, total_samp)
    gram = pl.pallas_call(
        gram_kernel,
        grid=(total_samp // tile,),
        out_shape=jax.ShapeDtypeStruct((extra, total_samp), jnp.float32),
        in_specs=[fixed(left.shape), fixed(linv.shape), fixed(lscale.shape),
                  pl.BlockSpec((tile, samples.shape[1]), lambda i: (i, 0)),
                  pl.BlockSpec((1, tile), lambda i: (0, i))],
        out_specs=pl.BlockSpec((extra, tile), lambda i: (0, i)),
        compiler_params=params,
    )(left, linv, lscale, samples, sscale[None, :])

    dma = pltpu.SemaphoreType.DMA
    block = (half, rows_dev)
    grad, grad_all = pl.pallas_call(
        functools.partial(sum_kernel, groups, rows),
        out_shape=[jax.ShapeDtypeStruct(block, jnp.float32),
                   jax.ShapeDtypeStruct((rows,) + block, jnp.float32)],
        in_specs=[VMEM, VMEM],
        out_specs=[VMEM, VMEM],
        scratch_shapes=[
            pltpu.VMEM((rows,) + block, jnp.float32),
            pltpu.VMEM((groups,) + block, jnp.float32),
            pltpu.VMEM(block, jnp.float32),
            dma((rows,)), dma((rows,)), dma((groups,)), dma((groups,)), dma((rows,)), dma((rows,)),
        ],
        compiler_params=pltpu.CompilerParams(
            collective_id=1, has_side_effects=True, vmem_limit_bytes=48 << 20),
    )(partial, jnp.pad(targets, ((0, half - labels), (0, 0))))
    gradient = grad[:labels]

    def times(a, b):
        return jnp.dot(a, b, precision=HIGH)

    push = sum(lax.dot_general(grad_all[i], cross[i], CONTRACT, precision=HIGH) for i in range(rows)) / total_rows
    if whole:
        factors = gathered[2].reshape(total_samp, -1)
        update = jnp.zeros_like(push)
        for step in range(PROJ_STEPS):
            slope = push if step == 0 else times(update, gram) / total_samp + push
            coef = times(slope, factors)
            update = update - (slope - lax.dot_general(coef, factors, CONTRACT, precision=HIGH))
        place = (lax.axis_index("row") * groups + lax.axis_index("centre")) * samp_dev
        return (gradient, lax.dynamic_slice(update, (0, place), (half, samp_dev))[:labels])
    push = push[:labels]
    update = jnp.zeros((labels, samp_dev), jnp.float32)
    for step in range(PROJ_STEPS):
        if step == 0:
            slope = push
        else:
            update_whole = lax.all_gather(update, ("row", "centre"), axis=1, tiled=True)
            slope = lax.dot_general(update_whole, gram, CONTRACT, precision=HIGH) / total_samp + push
        coef = lax.psum(times(slope, factor), ("centre", "row"))
        update = update - (slope - times(coef, factor.T))
    return (gradient, update)


def solution(mesh):
    placed = (
        P("centre", "row"),
        P("row"),
        P(None, "row"),
        P(("centre", "row"), None),
        P(None, ("centre", "row")),
        P(("centre", "row")),
        P(("centre", "row"), None),
    )
    return jax.shard_map(
        on_device,
        mesh=mesh,
        in_specs=placed,
        out_specs=(P(None, "row"), P(None, ("centre", "row"))),
        check_vma=False,
    )
```

```python
import functools
import math

import jax
import jax.numpy as jnp
from jax import lax
from jax.experimental import pallas as pl
from jax.experimental.pallas import tpu as pltpu
from jax.sharding import PartitionSpec as P

PROJ_STEPS = 2
EPS = 1e-06
HIGH = lax.Precision.HIGHEST
MESH = pl.DeviceIdType.MESH
CONTRACT = (((1,), (1,)), ((), ()))
VMEM = pl.BlockSpec(memory_space=pltpu.VMEM)
POLY = (0.3183098802, -0.8408441305, 0.09680761083, -0.03656900053,
        0.01880055716, -0.00968401399, 0.003746990699, -0.0007261497719)


def row_scale(rows, axis):
    values = rows.astype(jnp.float32)
    return jnp.sqrt(jnp.mean(values * values, axis=axis) + EPS)


def arc(cosine):
    size = jnp.minimum(jnp.abs(cosine), 1.0)
    rest = 1.0 - size
    root = rest * lax.rsqrt(jnp.maximum(rest, 1e-30))
    value = jnp.full_like(size, POLY[-1])
    for factor in POLY[-2::-1]:
        value = value * size + factor
    linear = jnp.minimum(jnp.maximum(cosine, 0.0), 1.0)
    return root * value + (linear + linear)


def pick_kernel(pool_ref, index_ref, out_ref):
    count = index_ref.shape[1]
    depth = pool_ref.shape[1]
    tile = 512
    total = jnp.zeros(out_ref.shape, jnp.float32)
    for start in range(0, depth, tile):
        size = min(tile, depth - start)
        wanted = index_ref[...] - start
        hot = lax.broadcasted_iota(jnp.int32, (size, count), 0) == wanted
        total += jnp.dot(pool_ref[:, start:start + size], hot.astype(jnp.bfloat16),
                         preferred_element_type=jnp.float32)
    out_ref[...] = total.astype(out_ref.dtype)


def fused_kernel(groups, rows, count, tile, whole, *refs):
    ins = refs[:count]
    cent_ref, inv_ref, weight_ref = refs[count:count + 3]
    refs = refs[count + 3:]
    part_ref, cross_ref = refs[:2]
    outs = (refs[count + 1],) + refs[2:count + 1]
    (scales, own, send1, recv1, send2, recv2, send3, recv3) = refs[count + 2:]
    width = cent_ref.shape[1]
    pairs = rows // 2
    c = lax.axis_index("centre")
    r = lax.axis_index("row")
    x, core = r // 2, r % 2
    other = r + 1 - 2 * core

    barrier = pltpu.get_barrier_semaphore()
    for d in range(1, groups):
        pl.semaphore_signal(barrier, inc=1, device_id=((c + d) % groups, r), device_id_type=MESH)
    for d in range(1, pairs):
        pl.semaphore_signal(barrier, inc=1, device_id=(c, ((x + d) % pairs) * 2 + core), device_id_type=MESH)
    pl.semaphore_signal(barrier, inc=1, device_id=(c, other), device_id_type=MESH)
    pl.semaphore_wait(barrier, groups - 1 + pairs - 1 + 1)

    def slot(a, row, centre):
        size = ins[a].shape[0]
        return outs[a].at[row, pl.ds(pl.multiple_of(centre * size, size), size), :]

    sent = []
    for a in range(count):
        for d in range(1, groups):
            to = (c + d) % groups
            copy = pltpu.make_async_remote_copy(
                ins[a], slot(a, r, c), send1.at[a, d], recv1.at[a, d],
                device_id=(to, r), device_id_type=MESH)
            copy.start()
            sent.append(copy)
    keep = []
    for a in range(count):
        copy = pltpu.make_async_copy(ins[a], slot(a, r, c), own.at[a])
        copy.start()
        keep.append(copy)
    for copy in keep:
        copy.wait()

    def forward(a, row, d, x_step):
        place = slot(a, row, (c + groups - d) % groups)
        copy = pltpu.make_async_remote_copy(
            place, place, send3.at[a, x_step, d], recv3.at[a, x_step, d],
            device_id=(c, other), device_id_type=MESH)
        copy.start()
        sent.append(copy)

    def here(a, d):
        place = slot(a, r, (c + groups - d) % groups)
        if d:
            pltpu.make_async_remote_copy(
                ins[a], place, send1.at[a, d], recv1.at[a, d],
                device_id=(c, r), device_id_type=MESH).wait_recv()
        for e in range(1, pairs):
            copy = pltpu.make_async_remote_copy(
                place, place, send2.at[a, e, d], recv2.at[a, e, d],
                device_id=(c, ((x + e) % pairs) * 2 + core), device_id_type=MESH)
            copy.start()
            sent.append(copy)
        forward(a, r, d, 0)

    def across(a, e):
        row = ((x + pairs - e) % pairs) * 2 + core
        for d in range(groups):
            place = slot(a, row, (c + groups - d) % groups)
            pltpu.make_async_remote_copy(
                place, place, send2.at[a, e, d], recv2.at[a, e, d],
                device_id=(c, r), device_id_type=MESH).wait_recv()
            forward(a, row, d, e)
        return row

    def paired(a, e):
        row = ((x + pairs - e) % pairs) * 2 + (1 - core)
        for d in range(groups):
            place = slot(a, row, (c + groups - d) % groups)
            pltpu.make_async_remote_copy(
                place, place, send3.at[a, e, d], recv3.at[a, e, d],
                device_id=(c, r), device_id_type=MESH).wait_recv()
        return row

    def block(row):
        batch = outs[0][row]
        exact = batch.astype(jnp.float32)
        bscale = jnp.sqrt(jnp.mean(exact * exact, axis=0, keepdims=True) + EPS)
        scales[row] = bscale
        binv = 1.0 / bscale
        half = weight_ref.shape[0]
        first = jnp.zeros((2 * half, batch.shape[1]), jnp.float32)
        second = jnp.zeros((half, batch.shape[1]), jnp.float32)
        for start in range(0, cent_ref.shape[0], tile):
            inner = jnp.dot(cent_ref[start:start + tile, :], batch, preferred_element_type=jnp.float32)
            value = arc(inner * inv_ref[start:start + tile, :] * binv)
            high = value.astype(jnp.bfloat16)
            low = (value - high.astype(jnp.float32)).astype(jnp.bfloat16)
            full = weight_ref[:, start:start + tile]
            upper = full.astype(jnp.bfloat16)
            lower = (full - upper.astype(jnp.float32)).astype(jnp.bfloat16)
            coeffs = jnp.concatenate([upper, lower], axis=0)
            first += jnp.dot(coeffs, high, preferred_element_type=jnp.float32)
            second += jnp.dot(upper, low, preferred_element_type=jnp.float32)
        part_ref[row] = (first[:half] + (first[half:] + second)) * bscale

    later = range(1, count)
    for d in range(groups):
        here(0, d)
    block(r)
    for a in later:
        for d in range(groups):
            here(a, d)
    block(paired(0, 0))
    for e in range(1, pairs):
        row = across(0, e)
        block(row)
        if e == pairs - 1:
            for a in later:
                paired(a, 0)
                for f in range(1, pairs):
                    across(a, f)
        block(paired(0, e))
    for a in later:
        for e in range(1, pairs):
            paired(a, e)

    for part in range(rows if whole else 1):
        left = outs[1][part] if whole else ins[1][...]
        exact = left.astype(jnp.float32)
        lscale = jnp.sqrt(jnp.mean(exact * exact, axis=1, keepdims=True) + EPS)
        linv = 1.0 / (width * lscale)
        size = left.shape[0]
        for row in range(rows):
            bscale = scales[row]
            inner = jnp.dot(left, outs[0][row], preferred_element_type=jnp.float32)
            value = arc(inner * linv * (1.0 / bscale))
            cross_ref[row, part * size:(part + 1) * size, :] = value * (lscale * bscale)
    for copy in sent:
        copy.wait_send()


def fused(groups, rows, arrays, centres, inv, scaled, whole):
    count = len(arrays)
    pairs = rows // 2
    dma = pltpu.SemaphoreType.DMA
    cols = arrays[0].shape[1]
    extra = arrays[1].shape[0] * (groups * rows if whole else 1)
    spread = [jax.ShapeDtypeStruct((rows, groups * a.shape[0], a.shape[1]), a.dtype) for a in arrays]
    return pl.pallas_call(
        functools.partial(fused_kernel, groups, rows, count, 512, whole),
        out_shape=[jax.ShapeDtypeStruct((rows, scaled.shape[0], cols), jnp.float32),
                   jax.ShapeDtypeStruct((rows, extra, cols), jnp.float32)] + spread[1:],
        in_specs=[VMEM] * (count + 3),
        out_specs=[VMEM] * (count + 1),
        scratch_shapes=[
            pltpu.VMEM(spread[0].shape, spread[0].dtype),
            pltpu.VMEM((rows, 1, cols), jnp.float32),
            dma((count,)),
            dma((count, groups)), dma((count, groups)),
            dma((count, pairs, groups)), dma((count, pairs, groups)),
            dma((count, pairs, groups)), dma((count, pairs, groups)),
        ],
        compiler_params=pltpu.CompilerParams(
            collective_id=0, has_side_effects=True, vmem_limit_bytes=48 << 20),
    )(*arrays, centres, inv, scaled)


def gram_kernel(left_ref, linv_ref, lscale_ref, right_ref, rscale_ref, out_ref):
    inner = lax.dot_general(left_ref[...], right_ref[...], CONTRACT, preferred_element_type=jnp.float32)
    rscale = rscale_ref[...]
    value = arc(inner * linv_ref[...] * (1.0 / rscale))
    out_ref[...] = value * (lscale_ref[...] * rscale)


def sum_kernel(groups, rows, part_ref, target_ref, grad_ref, all_ref, buf1, buf2, mine,
               send1, recv1, send2, recv2, send3, recv3):
    c = lax.axis_index("centre")
    r = lax.axis_index("row")
    barrier = pltpu.get_barrier_semaphore()
    for d in range(1, rows):
        pl.semaphore_signal(barrier, inc=1, device_id=(c, (r + d) % rows), device_id_type=MESH)
    for d in range(1, groups):
        pl.semaphore_signal(barrier, inc=1, device_id=((c + d) % groups, r), device_id_type=MESH)
    pl.semaphore_wait(barrier, rows - 1 + groups - 1)
    sent = []

    def move(src, dst, send, recv, to):
        copy = pltpu.make_async_remote_copy(src, dst, send, recv, device_id=to, device_id_type=MESH)
        copy.start()
        sent.append(copy)

    def landed(dst, send, recv):
        pltpu.make_async_remote_copy(dst, dst, send, recv, device_id=(c, r), device_id_type=MESH).wait_recv()

    for d in range(1, rows):
        to = (r + d) % rows
        move(part_ref.at[to], buf1.at[d], send1.at[d], recv1.at[d], (c, to))
    total = part_ref[r]
    for d in range(1, rows):
        landed(buf1.at[d], send1.at[d], recv1.at[d])
        total += buf1[d]
    mine[...] = total
    for d in range(1, groups):
        move(mine, buf2.at[c], send2.at[d], recv2.at[d], ((c + d) % groups, r))
    for d in range(1, groups):
        place = buf2.at[(c + groups - d) % groups]
        landed(place, send2.at[d], recv2.at[d])
    buf2[c] = total
    total = buf2[0]
    for d in range(1, groups):
        total += buf2[d]
    grad = total - target_ref[...]
    grad_ref[...] = grad
    all_ref[r] = grad
    for d in range(1, rows):
        move(grad_ref, all_ref.at[r], send3.at[d], recv3.at[d], (c, (r + d) % rows))
    for d in range(1, rows):
        landed(all_ref.at[(r + rows - d) % rows], send3.at[d], recv3.at[d])
    for copy in sent:
        copy.wait_send()


def on_device(pool, batch_index, targets, centres, weights, sample_index, factor):
    width = float(centres.shape[1])
    labels = weights.shape[0]
    rows_dev = batch_index.shape[0]
    pool_dev = pool.shape[1]
    cent_dev = centres.shape[0]
    samp_dev = sample_index.shape[0]
    rows = lax.axis_size("row")
    groups = lax.axis_size("centre")
    total_rows = rows_dev * rows
    total_samp = samp_dev * rows * groups
    whole = total_samp <= 1024
    half = -(-labels // 16) * 16
    params = pltpu.CompilerParams(vmem_limit_bytes=48 << 20)

    local_batch = batch_index - lax.axis_index("row") * pool_dev
    picked = pl.pallas_call(
        pick_kernel,
        out_shape=jax.ShapeDtypeStruct((pool.shape[0], rows_dev), pool.dtype),
        compiler_params=params,
    )(pool, local_batch[None, :])
    local_sample = sample_index - lax.axis_index(("centre", "row")) * cent_dev
    sample_rows = jnp.take(centres, local_sample, axis=0)
    arrays = [picked, sample_rows] + ([factor] if whole else [])
    centre_scale = row_scale(centres, 1)
    scaled = jnp.pad(weights * centre_scale[None, :], ((0, half - labels), (0, 0)))
    inv = (1.0 / (width * centre_scale))[:, None]
    partial, cross, *gathered = fused(groups, rows, arrays, centres, inv, scaled, whole)
    samples = gathered[0].reshape(total_samp, -1)
    sscale = row_scale(samples, 1)
    left = samples if whole else sample_rows
    lscale = (sscale if whole else row_scale(sample_rows, 1))[:, None]
    linv = 1.0 / (width * lscale)
    extra = left.shape[0]
    fixed = lambda shape: pl.BlockSpec(shape, lambda i: (0, 0))
    tile = min(512, total_samp)
    gram = pl.pallas_call(
        gram_kernel,
        grid=(total_samp // tile,),
        out_shape=jax.ShapeDtypeStruct((extra, total_samp), jnp.float32),
        in_specs=[fixed(left.shape), fixed(linv.shape), fixed(lscale.shape),
                  pl.BlockSpec((tile, samples.shape[1]), lambda i: (i, 0)),
                  pl.BlockSpec((1, tile), lambda i: (0, i))],
        out_specs=pl.BlockSpec((extra, tile), lambda i: (0, i)),
        compiler_params=params,
    )(left, linv, lscale, samples, sscale[None, :])

    dma = pltpu.SemaphoreType.DMA
    block = (half, rows_dev)
    grad, grad_all = pl.pallas_call(
        functools.partial(sum_kernel, groups, rows),
        out_shape=[jax.ShapeDtypeStruct(block, jnp.float32),
                   jax.ShapeDtypeStruct((rows,) + block, jnp.float32)],
        in_specs=[VMEM, VMEM],
        out_specs=[VMEM, VMEM],
        scratch_shapes=[
            pltpu.VMEM((rows,) + block, jnp.float32),
            pltpu.VMEM((groups,) + block, jnp.float32),
            pltpu.VMEM(block, jnp.float32),
            dma((rows,)), dma((rows,)), dma((groups,)), dma((groups,)), dma((rows,)), dma((rows,)),
        ],
        compiler_params=pltpu.CompilerParams(
            collective_id=1, has_side_effects=True, vmem_limit_bytes=48 << 20),
    )(partial, jnp.pad(targets, ((0, half - labels), (0, 0))))
    gradient = grad[:labels]

    def times(a, b):
        return jnp.dot(a, b, precision=HIGH)

    push = sum(lax.dot_general(grad_all[i], cross[i], CONTRACT, precision=HIGH) for i in range(rows)) / total_rows
    if whole:
        factors = gathered[1].reshape(total_samp, -1)
        update = jnp.zeros_like(push)
        for step in range(PROJ_STEPS):
            slope = push if step == 0 else times(update, gram) / total_samp + push
            coef = times(slope, factors)
            update = update - (slope - lax.dot_general(coef, factors, CONTRACT, precision=HIGH))
        place = (lax.axis_index("row") * groups + lax.axis_index("centre")) * samp_dev
        return (gradient, lax.dynamic_slice(update, (0, place), (half, samp_dev))[:labels])
    push = push[:labels]
    update = jnp.zeros((labels, samp_dev), jnp.float32)
    for step in range(PROJ_STEPS):
        if step == 0:
            slope = push
        else:
            update_whole = lax.all_gather(update, ("row", "centre"), axis=1, tiled=True)
            slope = lax.dot_general(update_whole, gram, CONTRACT, precision=HIGH) / total_samp + push
        coef = lax.psum(times(slope, factor), ("centre", "row"))
        update = update - (slope - times(coef, factor.T))
    return (gradient, update)


def solution(mesh):
    placed = (
        P("centre", "row"),
        P("row"),
        P(None, "row"),
        P(("centre", "row"), None),
        P(None, ("centre", "row")),
        P(("centre", "row")),
        P(("centre", "row"), None),
    )
    return jax.shard_map(
        on_device,
        mesh=mesh,
        in_specs=placed,
        out_specs=(P(None, "row"), P(None, ("centre", "row"))),
        check_vma=False,
    )
```

```python
import functools
import math

import jax
import jax.numpy as jnp
from jax import lax
from jax.experimental import pallas as pl
from jax.experimental.pallas import tpu as pltpu
from jax.sharding import PartitionSpec as P

PROJ_STEPS = 2
EPS = 1e-06
HIGH = lax.Precision.HIGHEST
MESH = pl.DeviceIdType.MESH
CONTRACT = (((1,), (1,)), ((), ()))
VMEM = pl.BlockSpec(memory_space=pltpu.VMEM)
POLY = (0.3183098418, -0.8408396621, 0.09672484892, -0.03600487561,
        0.01699589254, -0.006754446989, 0.00141088352)


def row_scale(rows, axis):
    values = rows.astype(jnp.float32)
    return jnp.sqrt(jnp.mean(values * values, axis=axis) + EPS)


def arc(cosine):
    size = jnp.minimum(jnp.abs(cosine), 1.0)
    rest = 1.0 - size
    root = rest * lax.rsqrt(jnp.maximum(rest, 1e-30))
    value = jnp.full_like(size, POLY[-1])
    for factor in POLY[-2::-1]:
        value = value * size + factor
    linear = jnp.minimum(jnp.maximum(cosine, 0.0), 1.0)
    return root * value + (linear + linear)


def pick_kernel(pool_ref, index_ref, out_ref):
    count = index_ref.shape[1]
    depth = pool_ref.shape[1]
    tile = 512
    total = jnp.zeros(out_ref.shape, jnp.float32)
    for start in range(0, depth, tile):
        size = min(tile, depth - start)
        wanted = index_ref[...] - start
        hot = lax.broadcasted_iota(jnp.int32, (size, count), 0) == wanted
        total += jnp.dot(pool_ref[:, start:start + size], hot.astype(jnp.bfloat16),
                         preferred_element_type=jnp.float32)
    out_ref[...] = total.astype(out_ref.dtype)


def rows_kernel(cent_ref, index_ref, out_ref, scale_ref):
    step = pl.program_id(0)
    tile = cent_ref.shape[0]
    rows = cent_ref[...]
    hot = lax.broadcasted_iota(jnp.int32, (index_ref.shape[0], tile), 1) + step * tile == index_ref[...]
    found = jnp.dot(hot.astype(jnp.bfloat16), rows, preferred_element_type=jnp.float32)

    @pl.when(step == 0)
    def _():
        out_ref[...] = jnp.zeros_like(out_ref)

    out_ref[...] = (out_ref[...].astype(jnp.float32) + found).astype(out_ref.dtype)
    exact = rows.astype(jnp.float32)
    scale_ref[...] = jnp.sqrt(jnp.mean(exact * exact, axis=1, keepdims=True) + EPS)


def fused_kernel(groups, rows, count, tile, whole, *refs):
    ins = refs[:count]
    cent_ref, inv_ref, weight_ref = refs[count:count + 3]
    refs = refs[count + 3:]
    part_ref, cross_ref = refs[:2]
    outs = (refs[count + 1],) + refs[2:count + 1]
    (scales, own, send1, recv1, send2, recv2, send3, recv3) = refs[count + 2:]
    width = cent_ref.shape[1]
    pairs = rows // 2
    c = lax.axis_index("centre")
    r = lax.axis_index("row")
    x, core = r // 2, r % 2
    other = r + 1 - 2 * core

    barrier = pltpu.get_barrier_semaphore()
    for d in range(1, groups):
        pl.semaphore_signal(barrier, inc=1, device_id=((c + d) % groups, r), device_id_type=MESH)
    for d in range(1, pairs):
        pl.semaphore_signal(barrier, inc=1, device_id=(c, ((x + d) % pairs) * 2 + core), device_id_type=MESH)
    pl.semaphore_signal(barrier, inc=1, device_id=(c, other), device_id_type=MESH)
    pl.semaphore_wait(barrier, groups - 1 + pairs - 1 + 1)

    def slot(a, row, centre):
        size = ins[a].shape[0]
        return outs[a].at[row, pl.ds(pl.multiple_of(centre * size, size), size), :]

    sent = []
    for a in range(count):
        for d in range(1, groups):
            to = (c + d) % groups
            copy = pltpu.make_async_remote_copy(
                ins[a], slot(a, r, c), send1.at[a, d], recv1.at[a, d],
                device_id=(to, r), device_id_type=MESH)
            copy.start()
            sent.append(copy)
    keep = []
    for a in range(count):
        copy = pltpu.make_async_copy(ins[a], slot(a, r, c), own.at[a])
        copy.start()
        keep.append(copy)
    for copy in keep:
        copy.wait()

    def forward(a, row, d, x_step):
        place = slot(a, row, (c + groups - d) % groups)
        copy = pltpu.make_async_remote_copy(
            place, place, send3.at[a, x_step, d], recv3.at[a, x_step, d],
            device_id=(c, other), device_id_type=MESH)
        copy.start()
        sent.append(copy)

    def here(a, d):
        place = slot(a, r, (c + groups - d) % groups)
        if d:
            pltpu.make_async_remote_copy(
                ins[a], place, send1.at[a, d], recv1.at[a, d],
                device_id=(c, r), device_id_type=MESH).wait_recv()
        for e in range(1, pairs):
            copy = pltpu.make_async_remote_copy(
                place, place, send2.at[a, e, d], recv2.at[a, e, d],
                device_id=(c, ((x + e) % pairs) * 2 + core), device_id_type=MESH)
            copy.start()
            sent.append(copy)
        forward(a, r, d, 0)

    def across(a, e):
        row = ((x + pairs - e) % pairs) * 2 + core
        for d in range(groups):
            place = slot(a, row, (c + groups - d) % groups)
            pltpu.make_async_remote_copy(
                place, place, send2.at[a, e, d], recv2.at[a, e, d],
                device_id=(c, r), device_id_type=MESH).wait_recv()
            forward(a, row, d, e)
        return row

    def paired(a, e):
        row = ((x + pairs - e) % pairs) * 2 + (1 - core)
        for d in range(groups):
            place = slot(a, row, (c + groups - d) % groups)
            pltpu.make_async_remote_copy(
                place, place, send3.at[a, e, d], recv3.at[a, e, d],
                device_id=(c, r), device_id_type=MESH).wait_recv()
        return row

    def block(row):
        batch = outs[0][row]
        exact = batch.astype(jnp.float32)
        bscale = jnp.sqrt(jnp.mean(exact * exact, axis=0, keepdims=True) + EPS)
        scales[row] = bscale
        binv = 1.0 / bscale
        half = weight_ref.shape[0]
        first = jnp.zeros((2 * half, batch.shape[1]), jnp.float32)
        second = jnp.zeros((half, batch.shape[1]), jnp.float32)
        for start in range(0, cent_ref.shape[0], tile):
            inner = jnp.dot(cent_ref[start:start + tile, :], batch, preferred_element_type=jnp.float32)
            value = arc(inner * inv_ref[start:start + tile, :] * binv)
            high = value.astype(jnp.bfloat16)
            low = (value - high.astype(jnp.float32)).astype(jnp.bfloat16)
            full = weight_ref[:, start:start + tile]
            upper = full.astype(jnp.bfloat16)
            lower = (full - upper.astype(jnp.float32)).astype(jnp.bfloat16)
            coeffs = jnp.concatenate([upper, lower], axis=0)
            first += jnp.dot(coeffs, high, preferred_element_type=jnp.float32)
            second += jnp.dot(upper, low, preferred_element_type=jnp.float32)
        part_ref[row] = (first[:half] + (first[half:] + second)) * bscale

    later = range(1, count)
    for d in range(groups):
        here(0, d)
    block(r)
    for a in later:
        for d in range(groups):
            here(a, d)
    block(paired(0, 0))
    for e in range(1, pairs):
        row = across(0, e)
        block(row)
        if e == pairs - 1:
            for a in later:
                paired(a, 0)
                for f in range(1, pairs):
                    across(a, f)
        block(paired(0, e))
    for a in later:
        for e in range(1, pairs):
            paired(a, e)

    for part in range(rows if whole else 1):
        left = outs[1][part] if whole else ins[1][...]
        exact = left.astype(jnp.float32)
        lscale = jnp.sqrt(jnp.mean(exact * exact, axis=1, keepdims=True) + EPS)
        linv = 1.0 / (width * lscale)
        size = left.shape[0]
        for row in range(rows):
            bscale = scales[row]
            inner = jnp.dot(left, outs[0][row], preferred_element_type=jnp.float32)
            value = arc(inner * linv * (1.0 / bscale))
            cross_ref[row, part * size:(part + 1) * size, :] = value * (lscale * bscale)
    for copy in sent:
        copy.wait_send()


def fused(groups, rows, arrays, centres, inv, scaled, whole):
    count = len(arrays)
    pairs = rows // 2
    dma = pltpu.SemaphoreType.DMA
    cols = arrays[0].shape[1]
    extra = arrays[1].shape[0] * (groups * rows if whole else 1)
    spread = [jax.ShapeDtypeStruct((rows, groups * a.shape[0], a.shape[1]), a.dtype) for a in arrays]
    return pl.pallas_call(
        functools.partial(fused_kernel, groups, rows, count, 512, whole),
        out_shape=[jax.ShapeDtypeStruct((rows, scaled.shape[0], cols), jnp.float32),
                   jax.ShapeDtypeStruct((rows, extra, cols), jnp.float32)] + spread[1:],
        in_specs=[VMEM] * (count + 3),
        out_specs=[VMEM] * (count + 1),
        scratch_shapes=[
            pltpu.VMEM(spread[0].shape, spread[0].dtype),
            pltpu.VMEM((rows, 1, cols), jnp.float32),
            dma((count,)),
            dma((count, groups)), dma((count, groups)),
            dma((count, pairs, groups)), dma((count, pairs, groups)),
            dma((count, pairs, groups)), dma((count, pairs, groups)),
        ],
        compiler_params=pltpu.CompilerParams(
            collective_id=0, has_side_effects=True, vmem_limit_bytes=48 << 20),
    )(*arrays, centres, inv, scaled)


def gram_kernel(left_ref, linv_ref, lscale_ref, right_ref, rscale_ref, out_ref):
    inner = lax.dot_general(left_ref[...], right_ref[...], CONTRACT, preferred_element_type=jnp.float32)
    rscale = rscale_ref[...]
    value = arc(inner * linv_ref[...] * (1.0 / rscale))
    out_ref[...] = value * (lscale_ref[...] * rscale)


def sum_kernel(groups, rows, part_ref, target_ref, grad_ref, all_ref, buf1, buf2, mine,
               send1, recv1, send2, recv2, send3, recv3):
    c = lax.axis_index("centre")
    r = lax.axis_index("row")
    barrier = pltpu.get_barrier_semaphore()
    for d in range(1, rows):
        pl.semaphore_signal(barrier, inc=1, device_id=(c, (r + d) % rows), device_id_type=MESH)
    for d in range(1, groups):
        pl.semaphore_signal(barrier, inc=1, device_id=((c + d) % groups, r), device_id_type=MESH)
    pl.semaphore_wait(barrier, rows - 1 + groups - 1)
    sent = []

    def move(src, dst, send, recv, to):
        copy = pltpu.make_async_remote_copy(src, dst, send, recv, device_id=to, device_id_type=MESH)
        copy.start()
        sent.append(copy)

    def landed(dst, send, recv):
        pltpu.make_async_remote_copy(dst, dst, send, recv, device_id=(c, r), device_id_type=MESH).wait_recv()

    for d in range(1, rows):
        to = (r + d) % rows
        move(part_ref.at[to], buf1.at[d], send1.at[d], recv1.at[d], (c, to))
    total = part_ref[r]
    for d in range(1, rows):
        landed(buf1.at[d], send1.at[d], recv1.at[d])
        total += buf1[d]
    mine[...] = total
    for d in range(1, groups):
        move(mine, buf2.at[c], send2.at[d], recv2.at[d], ((c + d) % groups, r))
    for d in range(1, groups):
        place = buf2.at[(c + groups - d) % groups]
        landed(place, send2.at[d], recv2.at[d])
    buf2[c] = total
    total = buf2[0]
    for d in range(1, groups):
        total += buf2[d]
    grad = total - target_ref[...]
    grad_ref[...] = grad
    all_ref[r] = grad
    for d in range(1, rows):
        move(grad_ref, all_ref.at[r], send3.at[d], recv3.at[d], (c, (r + d) % rows))
    for d in range(1, rows):
        landed(all_ref.at[(r + rows - d) % rows], send3.at[d], recv3.at[d])
    for copy in sent:
        copy.wait_send()


def on_device(pool, batch_index, targets, centres, weights, sample_index, factor):
    width = float(centres.shape[1])
    labels = weights.shape[0]
    rows_dev = batch_index.shape[0]
    pool_dev = pool.shape[1]
    cent_dev = centres.shape[0]
    samp_dev = sample_index.shape[0]
    rows = lax.axis_size("row")
    groups = lax.axis_size("centre")
    total_rows = rows_dev * rows
    total_samp = samp_dev * rows * groups
    whole = total_samp <= 1024
    half = -(-labels // 16) * 16
    params = pltpu.CompilerParams(vmem_limit_bytes=48 << 20)

    local_batch = batch_index - lax.axis_index("row") * pool_dev
    picked = pl.pallas_call(
        pick_kernel,
        out_shape=jax.ShapeDtypeStruct((pool.shape[0], rows_dev), pool.dtype),
        compiler_params=params,
    )(pool, local_batch[None, :])
    local_sample = sample_index - lax.axis_index(("centre", "row")) * cent_dev
    sample_rows, centre_scale = pl.pallas_call(
        rows_kernel,
        grid=(cent_dev // 512,),
        out_shape=[jax.ShapeDtypeStruct((samp_dev, centres.shape[1]), centres.dtype),
                   jax.ShapeDtypeStruct((cent_dev, 1), jnp.float32)],
        in_specs=[pl.BlockSpec((512, centres.shape[1]), lambda i: (i, 0)),
                  pl.BlockSpec((samp_dev, 1), lambda i: (0, 0))],
        out_specs=[pl.BlockSpec((samp_dev, centres.shape[1]), lambda i: (0, 0)),
                   pl.BlockSpec((512, 1), lambda i: (i, 0))],
        compiler_params=params,
    )(centres, local_sample[:, None])
    arrays = [picked, sample_rows] + ([factor] if whole else [])
    scaled = jnp.pad(weights * centre_scale.T, ((0, half - labels), (0, 0)))
    inv = 1.0 / (width * centre_scale)
    partial, cross, *gathered = fused(groups, rows, arrays, centres, inv, scaled, whole)
    samples = gathered[0].reshape(total_samp, -1)
    sscale = row_scale(samples, 1)
    left = samples if whole else sample_rows
    lscale = (sscale if whole else row_scale(sample_rows, 1))[:, None]
    linv = 1.0 / (width * lscale)
    extra = left.shape[0]
    fixed = lambda shape: pl.BlockSpec(shape, lambda i: (0, 0))
    tile = min(512, total_samp)
    gram = pl.pallas_call(
        gram_kernel,
        grid=(total_samp // tile,),
        out_shape=jax.ShapeDtypeStruct((extra, total_samp), jnp.float32),
        in_specs=[fixed(left.shape), fixed(linv.shape), fixed(lscale.shape),
                  pl.BlockSpec((tile, samples.shape[1]), lambda i: (i, 0)),
                  pl.BlockSpec((1, tile), lambda i: (0, i))],
        out_specs=pl.BlockSpec((extra, tile), lambda i: (0, i)),
        compiler_params=params,
    )(left, linv, lscale, samples, sscale[None, :])

    dma = pltpu.SemaphoreType.DMA
    block = (half, rows_dev)
    grad, grad_all = pl.pallas_call(
        functools.partial(sum_kernel, groups, rows),
        out_shape=[jax.ShapeDtypeStruct(block, jnp.float32),
                   jax.ShapeDtypeStruct((rows,) + block, jnp.float32)],
        in_specs=[VMEM, VMEM],
        out_specs=[VMEM, VMEM],
        scratch_shapes=[
            pltpu.VMEM((rows,) + block, jnp.float32),
            pltpu.VMEM((groups,) + block, jnp.float32),
            pltpu.VMEM(block, jnp.float32),
            dma((rows,)), dma((rows,)), dma((groups,)), dma((groups,)), dma((rows,)), dma((rows,)),
        ],
        compiler_params=pltpu.CompilerParams(
            collective_id=1, has_side_effects=True, vmem_limit_bytes=48 << 20),
    )(partial, jnp.pad(targets, ((0, half - labels), (0, 0))))
    gradient = grad[:labels]

    def times(a, b):
        return jnp.dot(a, b, precision=HIGH)

    push = sum(lax.dot_general(grad_all[i], cross[i], CONTRACT, precision=HIGH) for i in range(rows)) / total_rows
    if whole:
        factors = gathered[1].reshape(total_samp, -1)
        update = jnp.zeros_like(push)
        for step in range(PROJ_STEPS):
            slope = push if step == 0 else times(update, gram) / total_samp + push
            coef = times(slope, factors)
            update = update - (slope - lax.dot_general(coef, factors, CONTRACT, precision=HIGH))
        place = (lax.axis_index("row") * groups + lax.axis_index("centre")) * samp_dev
        return (gradient, lax.dynamic_slice(update, (0, place), (half, samp_dev))[:labels])
    push = push[:labels]
    update = jnp.zeros((labels, samp_dev), jnp.float32)
    for step in range(PROJ_STEPS):
        if step == 0:
            slope = push
        else:
            update_whole = lax.all_gather(update, ("row", "centre"), axis=1, tiled=True)
            slope = lax.dot_general(update_whole, gram, CONTRACT, precision=HIGH) / total_samp + push
        coef = lax.psum(times(slope, factor), ("centre", "row"))
        update = update - (slope - times(coef, factor.T))
    return (gradient, update)


def solution(mesh):
    placed = (
        P("centre", "row"),
        P("row"),
        P(None, "row"),
        P(("centre", "row"), None),
        P(None, ("centre", "row")),
        P(("centre", "row")),
        P(("centre", "row"), None),
    )
    return jax.shard_map(
        on_device,
        mesh=mesh,
        in_specs=placed,
        out_specs=(P(None, "row"), P(None, ("centre", "row"))),
        check_vma=False,
    )
```
